128 devices in a mesh: slab: 8 (over y_hi, z), view: 16 (over y_lo, x, core).
Axes of the slice: x: 4, y: 4 (y_hi: 2, y_lo: 2; y = y_hi * 2 + y_lo), z: 4, core: 2. Of those that a mesh axis runs over, the one named last changes fastest.
Arguments:
- volume: float32 [512, 65536], P('slab', 'view'), may hold values from 0 to 2
- sino: float32 [16, 128, 2048], P('view', 'slab'), may hold values from -6 to 6
- transaxial: bfloat16 [16, 256, 256, 256], P('view'), may hold values from -0.0625 to 0.0625
- blocks: int32 [16, 256], P('view'), may hold values from 0 to 7
- axial: bfloat16 [16, 512, 32], P('view', 'slab'), may hold values from -0.5 to 0.5
- band_start: int32 [16, 8], P('view', 'slab'), may hold values from 0 to 96, as said below
- band_len: int32 [16, 8], P('view', 'slab'), may hold values from 16 to 32, as said below
- row_weight: float32 [16, 128, 2048], P('view', 'slab'), may hold values from 0.25 to 2
- col_weight: float32 [512, 65536], P('slab', 'view'), may hold values from 0.25 to 1
Outputs:
- updated: float32 [512, 65536], P('slab', 'view')
- residual: float32 [16, 128, 2048], P('view', 'slab')
The draws below stay inside these ranges and needn't reach their ends.
Inputs may be any that keep to these rules, and one draw needn't show every extreme that they name: (s - 1) * 16 <= band_start[v, s] <= s * 16 for every slab s, band_start[v, 0] = 0, band_start[v, s] + band_len[v, s] <= min((s + 2) * 16, 128). In every view some slab has band_len = 32.
All inputs are finite; a program needn't handle non-finite values.
Results may differ from the reference program's by a relative error of at most 0.0019.
Values may be sent and summed in bfloat16 or wider, within the bound.
No kernel may reach another device: no remote copies, remote signals or barrier semaphores. Data moves between devices by JAX's collectives and lax.ppermute only.
A program may use at most 192 MiB of HBM per device.

```python
import math
import jax
import jax.numpy as jnp
from jax import lax

ZS = 64
NZ = 512
PT = 256
TILES = 256
NPIX = 65536
CB = 256
NCB = 8
DCOL = 2048
V = 16
RD = 16
ROWS = 128
BAND = 32
N_SLAB = 8


def draw_band_start(key, part):
    key = jax.random.fold_in(key, 11)
    slack = jax.random.randint(key, (V, N_SLAB), 0, RD // 2 + 1)
    slab_number = jnp.arange(N_SLAB, dtype=jnp.int32)[None, :]
    return jnp.clip(slab_number * RD - slack, 0, ROWS - BAND).astype(jnp.int32)


def draw_band_len(key, part):
    key = jax.random.fold_in(key, 23)
    lengths = jax.random.randint(key, (V, N_SLAB), RD, BAND + 1)
    longest = jnp.arange(N_SLAB, dtype=jnp.int32)[None, :] == jnp.arange(V, dtype=jnp.int32)[:, None] % N_SLAB
    return jnp.where(longest, BAND, lengths).astype(jnp.int32)


def place_ends(array, own_key, smallest, largest):
    spot = [jax.random.randint(jax.random.fold_in(own_key, axis), (), 0, length) for axis, length in enumerate(array.shape)]
    widest = array.shape.index(max(array.shape))
    next_to = spot[:widest] + [(spot[widest] + 1) % array.shape[widest]] + spot[widest + 1:]
    return array.at[tuple(spot)].set(smallest).at[tuple(next_to)].set(largest)


def level_of(key, shape, shards, smallest, largest):
    factor_of = 1.0
    for dim, shards_of in shards:
        heights = jax.random.uniform(jax.random.fold_in(jax.random.fold_in(key, 6), dim), (shards_of,), jnp.float32, smallest / len(shards), largest / len(shards))
        factor_of = factor_of * jnp.repeat(jnp.exp(heights), shape[dim] // shards_of).reshape((-1,) + (1,) * (len(shape) - 1 - dim))
    return factor_of


def scatter_about(rng, extent, width, reach, split=(), kind=jnp.bfloat16):
    drawn = jax.random.normal(rng, extent, jnp.float32) * width
    if len(split) > 0:
        drawn = level_of(rng, extent, split, -0.22, 0.18) * drawn
    return jnp.clip(drawn, min=-reach, max=reach).astype(kind)


def setup_inputs(seed: int = 0) -> dict:
    keys = jax.random.split(jax.random.key(seed), 10)
    return {
        "volume": jnp.clip(2.0 * jax.random.uniform(keys[0], (NZ, NPIX), jnp.float32) ** level_of(keys[0], (NZ, NPIX), ((0, 8), (1, 16)), -0.2, 0.2), 0.0, 2.0),
        "sino": scatter_about(keys[1], (V, ROWS, DCOL), 1.0, 6.0, ((0, 16), (1, 8)), jnp.float32),
        "transaxial": scatter_about(keys[2], (V, TILES, PT, CB), (TILES * PT // NCB) ** -0.5, 0.0625, ((0, 16),)),
        "blocks": place_ends(jax.random.randint(keys[3], (V, TILES), 0, NCB), jax.random.fold_in(keys[3], 1), 0, NCB - 1).astype(jnp.int32),
        "axial": scatter_about(keys[4], (V, NZ, BAND), (2 * ZS) ** -0.5, 0.5, ((0, 16), (1, 8))),
        "band_start": draw_band_start(jax.random.fold_in(keys[9], 71), 0),
        "band_len": draw_band_len(jax.random.fold_in(keys[9], 71), 0),
        "row_weight": jnp.clip(jnp.exp(math.log(2.0) - 2.0794415 * jax.random.uniform(keys[7], (V, ROWS, DCOL), jnp.float32) ** level_of(keys[7], (V, ROWS, DCOL), ((0, 16), (1, 8)), -0.2, 0.2)), 0.25, 2.0),
        "col_weight": jnp.clip(jnp.exp(math.log(1.0) - 1.3862944 * jax.random.uniform(keys[8], (NZ, NPIX), jnp.float32) ** level_of(keys[8], (NZ, NPIX), ((0, 8), (1, 16)), -0.2, 0.2)), 0.25, 1.0),
    }


HIGH = lax.Precision.HIGHEST


def reference(volume, sino, transaxial, blocks, axial, band_start, band_len, row_weight, col_weight):
    rounded = lax.optimization_barrier(volume.astype(jnp.bfloat16)).astype(jnp.float32)
    tiled = rounded.reshape(NZ, TILES, PT)
    selector = (blocks[:, :, None] == jnp.arange(NCB)[None, None, :]).astype(jnp.float32)

    def project_view(inputs):
        weights, chooser = inputs
        per_tile = jnp.einsum("zti,tik->tzk", tiled, weights.astype(jnp.float32), precision=HIGH)
        return jnp.einsum("tc,tzk->zck", chooser, per_tile, precision=HIGH).reshape(NZ, DCOL)

    projected = lax.map(project_view, (transaxial, selector))
    live_rows = (jnp.arange(BAND)[None, None, :] < band_len[:, :, None]).astype(jnp.float32)
    masked = axial.astype(jnp.float32).reshape(V, N_SLAB, ZS, BAND) * live_rows[:, :, None, :]
    band_proj = jnp.einsum("vszj,vszu->vsju", masked, projected.reshape(V, N_SLAB, ZS, DCOL), precision=HIGH)
    placing = (band_start[:, :, None, None] + jnp.arange(BAND)[None, None, :, None]
               == jnp.arange(ROWS)[None, None, None, :]).astype(jnp.float32)
    forward = jnp.einsum("vsjr,vsju->vru", placing, band_proj, precision=HIGH)
    residual = row_weight * (sino - forward)
    band_res = jnp.einsum("vsjr,vru->vsju", placing, residual, precision=HIGH)
    smeared = jnp.einsum("vszj,vsju->vszu", masked, band_res, precision=HIGH).reshape(V, NZ, NCB, CB)
    rounded_back = lax.optimization_barrier(smeared.astype(jnp.bfloat16)).astype(jnp.float32)

    def back_view(running, inputs):
        weights, chooser, spread = inputs
        pulled = jnp.einsum("tc,zck->tzk", chooser, spread, precision=HIGH)
        return running + jnp.einsum("tik,tzk->zti", weights.astype(jnp.float32), pulled, precision=HIGH), None

    summed, unused = lax.scan(back_view, jnp.zeros((NZ, TILES, PT), jnp.float32),
                              (transaxial, selector, rounded_back))
    updated = jnp.maximum(volume + col_weight * summed.reshape(NZ, NPIX), 0.0)
    return updated, residual
```

```python
import functools
import jax
import jax.numpy as jnp
from jax import lax
from jax.experimental import pallas as pl
from jax.experimental.pallas import tpu as pltpu
from jax.sharding import PartitionSpec as P

F32 = jnp.float32
BF16 = jnp.bfloat16
MIB = 2**20
VM = pl.BlockSpec(memory_space=pltpu.VMEM)
SM = pl.BlockSpec(memory_space=pltpu.SMEM)
ANY = pl.BlockSpec(memory_space=pl.ANY)
HBM = pl.BlockSpec(memory_space=pltpu.HBM)
NT = (((1,), (1,)), ((), ()))
NX = 4


def place(y, x, c):
    return (y % 2) * 2 * NX + (x % NX) * 2 + c


def moves(step):
    return [
        (place(y, x, c), place(*step(y, x, c)))
        for y in range(2)
        for x in range(NX)
        for c in range(2)
    ]


UP = moves(lambda y, x, c: (y, x + 1, c))
DOWN = moves(lambda y, x, c: (y, x - 1, c))
ACROSS = moves(lambda y, x, c: (y + 1, x, c))
CORE = moves(lambda y, x, c: (y, x, 1 - c))


def send(array, pairs):
    return lax.ppermute(array, "view", pairs)


def params(mib):
    return pltpu.CompilerParams(vmem_limit_bytes=mib * MIB)


def split(value):
    high = value.astype(BF16)
    return high, (value - high.astype(F32)).astype(BF16)


def dot(a, b):
    return jnp.dot(a, b, preferred_element_type=F32)


def base_of(info, dx, dy, other, tiles):
    view = info[0]
    y, x, c = view // (2 * NX), (view // 2) % NX, view % 2
    c = 1 - c if other else c
    owner = lax.rem(y + dy, 2) * 2 * NX + lax.rem(x + dx + NX, NX) * 2 + c
    return owner * tiles


def cheap():
    return pl.CostEstimate(flops=1, bytes_accessed=1, transcendentals=0)


def cost(chunks):
    return pl.CostEstimate(
        flops=int(chunks * 3.4e8), bytes_accessed=int(chunks * 6e5), transcendentals=0
    )


def round_volume(volume, info):
    def body(source, about, out):
        out[...] = source[...].astype(BF16)

    return pl.pallas_call(
        body,
        in_specs=[VM, SM],
        out_specs=VM,
        out_shape=jax.ShapeDtypeStruct(volume.shape, BF16),
        compiler_params=params(12),
        cost_estimate=cheap(),
        name="round_volume",
    )(volume, info)


def gate(arrays, after):
    n = len(arrays)

    def body(*refs):
        pass

    return pl.pallas_call(
        body,
        in_specs=[ANY] * (n + 1),
        out_specs=[ANY] * n,
        out_shape=[jax.ShapeDtypeStruct(a.shape, a.dtype) for a in arrays],
        input_output_aliases={i: i for i in range(n)},
        compiler_params=params(12),
        cost_estimate=cheap(),
        name="gate",
    )(*arrays, after)


def cut(array, start, size, after):
    def body(source, earlier, out):
        out[...] = source[:, start : start + size]

    return pl.pallas_call(
        body,
        in_specs=[VM, ANY],
        out_specs=VM,
        out_shape=jax.ShapeDtypeStruct((array.shape[0], size), array.dtype),
        compiler_params=params(12),
        cost_estimate=cheap(),
        name="cut",
    )(array, after)


def join(low, high, after):
    size = low.shape[1]

    def body(a, b, earlier, out):
        out[:, :size] = a[...]
        out[:, size:] = b[...]

    return pl.pallas_call(
        body,
        in_specs=[VM, VM, ANY],
        out_specs=VM,
        out_shape=jax.ShapeDtypeStruct((low.shape[0], 2 * size), low.dtype),
        compiler_params=params(12),
        cost_estimate=cheap(),
        name="join",
    )(low, high, after)


def load_footprints(source, after):
    pieces = 16
    each = source.shape[0] // pieces

    def body(src, earlier, target, sems):
        copies = [
            pltpu.make_async_copy(
                src.at[pl.ds(i * each, each)], target.at[pl.ds(i * each, each)], sems.at[i]
            )
            for i in range(pieces)
        ]
        for copy in copies:
            copy.start()
        for copy in copies:
            copy.wait()

    return pl.pallas_call(
        body,
        in_specs=[HBM, ANY],
        out_specs=VM,
        out_shape=pltpu.VMEM(source.shape, source.dtype),
        scratch_shapes=[pltpu.SemaphoreType.DMA((pieces,))],
        compiler_params=params(12),
        cost_estimate=pl.CostEstimate(flops=1, bytes_accessed=source.size * 2, transcendentals=0),
        name="load_footprints",
    )(source, after)


def placing(info, axial):
    most, planes = axial.shape
    window = 48
    first, length = info[1], info[2]
    live = lax.broadcasted_iota(jnp.int32, (most, planes), 0) < length
    masked = jnp.where(live, axial[...].astype(F32), 0.0).astype(BF16)
    hot = (
        lax.broadcasted_iota(jnp.int32, (window, most), 1) + first
        == lax.broadcasted_iota(jnp.int32, (window, most), 0)
    )
    return dot(jnp.where(hot, 1.0, 0.0).astype(BF16), masked)


def project(weights, blocks, info, places, shards, total=None, axial=None):
    planes, pixels = shards[0].shape
    width, columns = weights.shape[1], weights.shape[2]
    tiles = pixels // width
    detector = 8 * columns
    n = len(shards)
    started = total is not None
    last = axial is not None
    piece = 4
    pieces = tiles // piece

    def body(blk, about, w, *refs):
        refs = list(refs)
        parts = [refs.pop(0) for _ in range(n)]
        before = refs.pop(0) if started else None
        ax = refs.pop(0) if last else None
        outs = [refs.pop(0) for _ in range(3)] if last else None
        acc, slots, sems = refs
        origins = [base_of(about, *places[p], tiles) for p in range(n)]
        copies = [
            pltpu.make_async_copy(
                w.at[pl.ds(origins[p] + q * piece, piece)],
                slots.at[pl.ds(p * tiles + q * piece, piece)],
                sems.at[p * pieces + q],
            )
            for p in range(n)
            for q in range(pieces)
        ]
        for copy in copies:
            copy.start()
        acc[...] = before[...] if started else jnp.zeros(acc.shape, F32)
        for p in range(n):
            for q in range(pieces):
                copies[p * pieces + q].wait()
                for i in range(q * piece, (q + 1) * piece):
                    at = pl.multiple_of(blk[0, origins[p] + i] * columns, columns)
                    row = parts[p][:, i * width : (i + 1) * width]
                    acc[:, pl.ds(at, columns)] += dot(row, slots[p * tiles + i])
        if last:
            placed = placing(about, ax).astype(BF16)
            high, low = split(acc[...])
            spread = dot(placed, high) + dot(placed, low)
            for k in range(3):
                outs[k][...] = spread[16 * k : 16 * k + 16]

    args = [blocks, info, weights, *shards]
    specs = [SM, SM, HBM] + [VM] * n
    if started:
        args.append(total)
        specs.append(VM)
    scratch = [
        pltpu.VMEM((n * tiles, width, columns), BF16),
        pltpu.SemaphoreType.DMA((n * pieces,)),
    ]
    if last:
        args.append(axial)
        specs.append(VM)
        out_shape = [jax.ShapeDtypeStruct((16, detector), F32)] * 3
        out_specs = [VM] * 3
        scratch = [pltpu.VMEM((planes, detector), F32)] + scratch
    else:
        out_shape = jax.ShapeDtypeStruct((planes, detector), F32)
        out_specs = VM
    return pl.pallas_call(
        body,
        in_specs=specs,
        out_specs=out_specs,
        out_shape=out_shape,
        scratch_shapes=scratch,
        compiler_params=params(2 * n + 4),
        cost_estimate=cost(n),
        name="project",
    )(*args)


def weigh(row_weight, sino, mine, low, high):
    def body(rw, measured, a, b, c, out, short):
        value = rw[0] * (measured[0] - (a[...] + b[...] + c[...]))
        out[...] = value
        short[...] = value.astype(BF16)

    return pl.pallas_call(
        body,
        in_specs=[VM] * 5,
        out_specs=[VM, VM],
        out_shape=[
            jax.ShapeDtypeStruct(mine.shape, F32),
            jax.ShapeDtypeStruct(mine.shape, BF16),
        ],
        compiler_params=params(12),
        cost_estimate=cheap(),
        name="weigh",
    )(row_weight, sino, mine, low, high)


def smear(info, axial, rows):
    planes = axial.shape[1]
    detector = rows[0].shape[1]

    def body(about, ax, low_rows, own_rows, high_rows, out):
        placed = placing(about, ax).T.astype(BF16)
        window = jnp.concatenate(
            [low_rows[...].astype(F32), own_rows[...], high_rows[...].astype(F32)], axis=0
        )
        high, low = split(window)
        out[...] = (dot(placed, high) + dot(placed, low)).astype(BF16)

    return pl.pallas_call(
        body,
        in_specs=[SM, VM, VM, VM, VM],
        out_specs=VM,
        out_shape=jax.ShapeDtypeStruct((planes, detector), BF16),
        compiler_params=params(12),
        cost_estimate=cheap(),
        name="smear",
    )(info, axial, *rows)


def pull(weights, blocks, info, places, smeared, adds=None, after=(), out_dtype=F32, joined=False):
    width, columns = weights.shape[1], weights.shape[2]
    planes = smeared.shape[0]
    tiles = weights.shape[0] // (4 * NX)
    pixels = tiles * width
    n = len(places)
    adds = adds or []
    sources = list({id(array): array for array, _ in adds}.values())
    piece = 8
    pieces = tiles // piece

    def body(blk, about, w, sm, *refs):
        given = dict(zip([id(a) for a in sources], refs[: len(sources)]))
        outs = refs[len(sources) + len(after) : -2]
        slots, sems = refs[-2:]
        origins = [base_of(about, *places[p], tiles) for p in range(n)]
        copies = [
            pltpu.make_async_copy(
                w.at[pl.ds(origins[p] + q * piece, piece)],
                slots.at[pl.ds(p * tiles + q * piece, piece)],
                sems.at[p * pieces + q],
            )
            for p in range(n)
            for q in range(pieces)
        ]
        for copy in copies:
            copy.start()
        for p in range(n):
            out, shift = (outs[0], p * pixels) if joined else (outs[p], 0)
            for q in range(pieces):
                copies[p * pieces + q].wait()
                for i in range(q * piece, (q + 1) * piece):
                    at = pl.multiple_of(blk[0, origins[p] + i] * columns, columns)
                    value = lax.dot_general(
                        sm[:, pl.ds(at, columns)],
                        slots[p * tiles + i],
                        NT,
                        preferred_element_type=F32,
                    )
                    if adds:
                        array, first = adds[p]
                        first += i * width
                        value += given[id(array)][:, first : first + width].astype(F32)
                    out[:, shift + i * width : shift + (i + 1) * width] = value.astype(out.dtype)

    shapes = [(planes, n * pixels)] if joined else [(planes, pixels)] * n
    out = pl.pallas_call(
        body,
        in_specs=[SM, SM, HBM, VM] + [VM] * len(sources) + [ANY] * len(after),
        out_specs=[VM] * len(shapes),
        out_shape=[jax.ShapeDtypeStruct(shape, out_dtype) for shape in shapes],
        scratch_shapes=[
            pltpu.VMEM((n * tiles, width, columns), BF16),
            pltpu.SemaphoreType.DMA((n * pieces,)),
        ],
        compiler_params=params(24),
        cost_estimate=cost(n),
        name="pull",
    )(blocks, info, weights, smeared, *sources, *after)
    return out[0] if joined else out


def combine(sums, size, cuts=1, after=()):
    arrays = list({id(term[0]): term[0] for terms in sums for term in terms}.values())
    half = size // 2
    planes = arrays[0].shape[0]

    def body(*refs):
        given = dict(zip([id(a) for a in arrays], refs[: len(arrays)]))
        outs = refs[len(arrays) + len(after) :]
        for s, terms in enumerate(sums):
            for h in range(2):
                value = None
                for array, first, halves in terms:
                    if h in halves:
                        first += h * half
                        more = given[id(array)][:, first : first + half].astype(F32)
                        value = more if value is None else value + more
                if cuts == 2:
                    outs[2 * s + h][...] = value.astype(BF16)
                else:
                    outs[s][:, h * half : (h + 1) * half] = value.astype(BF16)

    return pl.pallas_call(
        body,
        in_specs=[VM] * len(arrays) + [ANY] * len(after),
        out_specs=[VM] * (len(sums) * cuts),
        out_shape=[jax.ShapeDtypeStruct((planes, size // cuts), BF16)] * (len(sums) * cuts),
        compiler_params=params(16),
        cost_estimate=cheap(),
        name="combine",
    )(*arrays, *after)


def update(volume, col_weight, kept, swap, arrived):
    def body(vol, weight, mine, d, a, b, c, out):
        summed = mine[...] + d[...].astype(F32) + a[...].astype(F32) + b[...].astype(F32) + c[...].astype(F32)
        out[...] = jnp.maximum(vol[...] + weight[...] * summed, 0.0)

    planes, pixels = volume.shape
    block = pl.BlockSpec((planes, pixels // 4), lambda i: (0, i))
    return pl.pallas_call(
        body,
        grid=(4,),
        in_specs=[block] * 7,
        out_specs=block,
        out_shape=jax.ShapeDtypeStruct(volume.shape, F32),
        compiler_params=params(12),
        name="update",
    )(
        volume,
        col_weight,
        kept,
        swap,
        *arrived,
    )


def per_device(
    volume, sino, transaxial, blocks, axial, band_start, band_len, row_weight, col_weight
):
    planes, pixels = volume.shape
    rows_here = sino.shape[1]
    half = pixels // 2
    ax = jnp.swapaxes(axial[0], 0, 1)
    slab = lax.axis_index("slab")
    view = lax.axis_index("view")
    first = band_start[0, 0] - (slab - 1) * rows_here
    info = jnp.stack([view, first, band_len[0, 0]]).astype(jnp.int32)

    def whose(dx, dy):
        return [(dx, dy, False), (dx, dy, True)]

    own = round_volume(volume, info)
    left = send(own, UP)
    right = send(own, DOWN)
    over = send(own, ACROSS)
    swapped = send(own, CORE)
    weights = pltpu.with_memory_space_constraint(transaxial[0], pltpu.HBM)
    ahead = functools.partial(project, weights, blocks, info)
    total = ahead(whose(0, 0), [own, swapped])
    left, right, over = gate([left, right, over], total)
    far_low = send(cut(left, 0, half, total), UP)
    far_high = send(cut(right, half, half, total), DOWN)
    left_over = send(over, UP)
    right_over = send(over, DOWN)
    total = ahead(
        whose(-1, 0) + whose(1, 0), [left, send(left, CORE), right, send(right, CORE)], total
    )
    far = join(far_low, far_high, total)
    far_over = send(far, ACROSS)
    t1 = total
    left_over, right_over = gate([left_over, right_over], t1)
    total = ahead(whose(0, 1) + whose(2, 0), [over, send(over, CORE), far, send(far, CORE)], total)
    t2 = total
    total = ahead(
        whose(-1, 1) + whose(1, 1),
        [left_over, send(left_over, CORE), right_over, send(right_over, CORE)],
        total,
    )
    (far_over,) = gate([far_over], t2)
    below, mine, above = ahead(whose(2, 1), [far_over, send(far_over, CORE)], total, ax)

    count = lax.axis_size("slab")
    rise = [(i, i + 1) for i in range(count - 1)]
    fall = [(i + 1, i) for i in range(count - 1)]
    residual, rounded = weigh(
        row_weight, sino, mine, lax.ppermute(above, "slab", rise), lax.ppermute(below, "slab", fall)
    )
    low_rows = lax.ppermute(rounded, "slab", rise)
    high_rows = lax.ppermute(rounded, "slab", fall)
    smeared = smear(info, ax, [low_rows, residual, high_rows])

    back = functools.partial(pull, weights, blocks, info)
    full = (0, 1)

    def others(*offsets):
        return [(dx, dy, True) for dx, dy in offsets]

    def owns(*offsets):
        return [(dx, dy, False) for dx, dy in offsets]

    def rounds(offsets, after):
        parts = back(others(*offsets), smeared, after=after, out_dtype=BF16)
        swaps = [send(part, CORE) for part in parts]
        mine = back(owns(*offsets), smeared, after=[parts[0]])
        return [[(a, 0, full), (b, 0, full)] for a, b in zip(mine, swaps)]

    far_sum, up_sum, down_sum = combine(rounds([(2, 1), (1, 1), (-1, 1)], []), pixels)
    from_over = send(far_sum, ACROSS)
    from_left = send(up_sum, UP)
    from_right = send(down_sum, DOWN)
    to_far, to_over = rounds([(2, 0), (0, 1)], [far_sum])
    half_up, half_down = combine([to_far + [(from_over, 0, full)]], pixels, 2)
    half_left = send(half_up, UP)
    half_right = send(half_down, DOWN)
    (over_sum,) = combine(
        [to_over + [(from_left, 0, full), (from_right, 0, full)]], pixels, after=[half_up]
    )
    over_last = send(over_sum, ACROSS)
    to_up, to_down, here = rounds([(1, 0), (-1, 0), (0, 0)], [over_sum])
    up_sum, down_sum = combine(
        [to_up + [(half_left, 0, (0,))], to_down + [(half_right, -half, (1,))]], pixels
    )
    left_last = send(up_sum, UP)
    right_last = send(down_sum, DOWN)
    updated = update(
        volume, col_weight, here[0][0], here[1][0], [over_last, left_last, right_last]
    )
    return updated, residual[None]


def solution(mesh):
    in_specs = (
        P("slab", "view"),
        P("view", "slab", None),
        P("view", None, None, None),
        P("view", None),
        P("view", "slab", None),
        P("view", "slab"),
        P("view", "slab"),
        P("view", "slab", None),
        P("slab", "view"),
    )
    out_specs = (P("slab", "view"), P("view", "slab", None))
    return jax.shard_map(
        per_device, mesh=mesh, in_specs=in_specs, out_specs=out_specs, check_vma=False
    )
```

```python
import functools
import jax
import jax.numpy as jnp
from jax import lax
from jax.experimental import pallas as pl
from jax.experimental.pallas import tpu as pltpu
from jax.sharding import PartitionSpec as P

F32 = jnp.float32
BF16 = jnp.bfloat16
MIB = 2**20
VM = pl.BlockSpec(memory_space=pltpu.VMEM)
SM = pl.BlockSpec(memory_space=pltpu.SMEM)
ANY = pl.BlockSpec(memory_space=pl.ANY)
HBM = pl.BlockSpec(memory_space=pltpu.HBM)
NT = (((1,), (1,)), ((), ()))
NX = 4


def place(y, x, c):
    return (y % 2) * 2 * NX + (x % NX) * 2 + c


def moves(step):
    return [
        (place(y, x, c), place(*step(y, x, c)))
        for y in range(2)
        for x in range(NX)
        for c in range(2)
    ]


UP = moves(lambda y, x, c: (y, x + 1, c))
DOWN = moves(lambda y, x, c: (y, x - 1, c))
ACROSS = moves(lambda y, x, c: (y + 1, x, c))
CORE = moves(lambda y, x, c: (y, x, 1 - c))


def send(array, pairs):
    return lax.ppermute(array, "view", pairs)


def params(mib):
    return pltpu.CompilerParams(vmem_limit_bytes=mib * MIB)


def split(value):
    high = value.astype(BF16)
    return high, (value - high.astype(F32)).astype(BF16)


def dot(a, b):
    return jnp.dot(a, b, preferred_element_type=F32)


def base_of(info, dx, dy, other, tiles):
    view = info[0]
    y, x, c = view // (2 * NX), (view // 2) % NX, view % 2
    c = 1 - c if other else c
    owner = lax.rem(y + dy, 2) * 2 * NX + lax.rem(x + dx + NX, NX) * 2 + c
    return owner * tiles


def cheap():
    return pl.CostEstimate(flops=1, bytes_accessed=1, transcendentals=0)


def round_volume(volume, info):
    def body(source, about, out):
        out[...] = source[...].astype(BF16)

    return pl.pallas_call(
        body,
        in_specs=[VM, SM],
        out_specs=VM,
        out_shape=jax.ShapeDtypeStruct(volume.shape, BF16),
        compiler_params=params(12),
        cost_estimate=cheap(),
        name="round_volume",
    )(volume, info)


def gate(arrays, after):
    n = len(arrays)

    def body(*refs):
        pass

    return pl.pallas_call(
        body,
        in_specs=[ANY] * (n + 1),
        out_specs=[ANY] * n,
        out_shape=[jax.ShapeDtypeStruct(a.shape, a.dtype) for a in arrays],
        input_output_aliases={i: i for i in range(n)},
        compiler_params=params(12),
        cost_estimate=cheap(),
        name="gate",
    )(*arrays, after)


def cut(array, start, size, after):
    def body(source, earlier, out):
        out[...] = source[:, start : start + size]

    return pl.pallas_call(
        body,
        in_specs=[VM, ANY],
        out_specs=VM,
        out_shape=jax.ShapeDtypeStruct((array.shape[0], size), array.dtype),
        compiler_params=params(12),
        cost_estimate=cheap(),
        name="cut",
    )(array, after)


def join(low, high, after):
    size = low.shape[1]

    def body(a, b, earlier, out):
        out[:, :size] = a[...]
        out[:, size:] = b[...]

    return pl.pallas_call(
        body,
        in_specs=[VM, VM, ANY],
        out_specs=VM,
        out_shape=jax.ShapeDtypeStruct((low.shape[0], 2 * size), low.dtype),
        compiler_params=params(12),
        cost_estimate=cheap(),
        name="join",
    )(low, high, after)


def load_footprints(source, after):
    pieces = 16
    each = source.shape[0] // pieces

    def body(src, earlier, target, sems):
        copies = [
            pltpu.make_async_copy(
                src.at[pl.ds(i * each, each)], target.at[pl.ds(i * each, each)], sems.at[i]
            )
            for i in range(pieces)
        ]
        for copy in copies:
            copy.start()
        for copy in copies:
            copy.wait()

    return pl.pallas_call(
        body,
        in_specs=[HBM, ANY],
        out_specs=VM,
        out_shape=pltpu.VMEM(source.shape, source.dtype),
        scratch_shapes=[pltpu.SemaphoreType.DMA((pieces,))],
        compiler_params=params(12),
        cost_estimate=pl.CostEstimate(flops=1, bytes_accessed=source.size * 2, transcendentals=0),
        name="load_footprints",
    )(source, after)


def placing(info, axial):
    most, planes = axial.shape
    window = 48
    first, length = info[1], info[2]
    live = lax.broadcasted_iota(jnp.int32, (most, planes), 0) < length
    masked = jnp.where(live, axial[...].astype(F32), 0.0).astype(BF16)
    hot = (
        lax.broadcasted_iota(jnp.int32, (window, most), 1) + first
        == lax.broadcasted_iota(jnp.int32, (window, most), 0)
    )
    return dot(jnp.where(hot, 1.0, 0.0).astype(BF16), masked)


def project(weights, blocks, info, places, shards, total=None, axial=None):
    planes, pixels = shards[0].shape
    width, columns = weights.shape[1], weights.shape[2]
    tiles = pixels // width
    detector = 8 * columns
    n = len(shards)
    started = total is not None
    last = axial is not None
    piece = 4
    pieces = tiles // piece

    def body(blk, about, w, *refs):
        refs = list(refs)
        parts = [refs.pop(0) for _ in range(n)]
        before = refs.pop(0) if started else None
        ax = refs.pop(0) if last else None
        outs = [refs.pop(0) for _ in range(3)] if last else None
        acc, slots, sems = refs
        origins = [base_of(about, *places[p], tiles) for p in range(n)]
        copies = [
            pltpu.make_async_copy(
                w.at[pl.ds(origins[p] + q * piece, piece)],
                slots.at[pl.ds(p * tiles + q * piece, piece)],
                sems.at[p * pieces + q],
            )
            for p in range(n)
            for q in range(pieces)
        ]
        for copy in copies:
            copy.start()
        acc[...] = before[...] if started else jnp.zeros(acc.shape, F32)
        for p in range(n):
            for q in range(pieces):
                copies[p * pieces + q].wait()
                for i in range(q * piece, (q + 1) * piece):
                    at = pl.multiple_of(blk[0, origins[p] + i] * columns, columns)
                    row = parts[p][:, i * width : (i + 1) * width]
                    acc[:, pl.ds(at, columns)] += dot(row, slots[p * tiles + i])
        if last:
            placed = placing(about, ax).astype(BF16)
            high, low = split(acc[...])
            spread = dot(placed, high) + dot(placed, low)
            outs[1][...] = spread[16:32]
            odd = lax.rem(about[3], 2)

            @pl.when(odd == 1)
            def _():
                outs[0][...] = spread[32:]
                outs[2][...] = spread[:16]

            @pl.when(odd == 0)
            def _():
                outs[0][...] = spread[:16]
                outs[2][...] = spread[32:]

    args = [blocks, info, weights, *shards]
    specs = [SM, SM, HBM] + [VM] * n
    if started:
        args.append(total)
        specs.append(VM)
    scratch = [
        pltpu.VMEM((n * tiles, width, columns), BF16),
        pltpu.SemaphoreType.DMA((n * pieces,)),
    ]
    if last:
        args.append(axial)
        specs.append(VM)
        out_shape = [jax.ShapeDtypeStruct((16, detector), F32)] * 3
        out_specs = [VM] * 3
        scratch = [pltpu.VMEM((planes, detector), F32)] + scratch
    else:
        out_shape = jax.ShapeDtypeStruct((planes, detector), F32)
        out_specs = VM
    return pl.pallas_call(
        body,
        in_specs=specs,
        out_specs=out_specs,
        out_shape=out_shape,
        scratch_shapes=scratch,
        compiler_params=params(2 * n + 4),
        cost_estimate=cheap(),
        name="project",
    )(*args)


def weigh(row_weight, sino, mine, low, high):
    def body(rw, measured, a, b, c, out, again, short):
        value = rw[0] * (measured[0] - (a[...] + b[...] + c[...]))
        out[...] = value
        again[...] = value
        short[...] = value.astype(BF16)

    return pl.pallas_call(
        body,
        in_specs=[VM] * 5,
        out_specs=[VM] * 3,
        out_shape=[jax.ShapeDtypeStruct(mine.shape, F32)] * 2
        + [
            jax.ShapeDtypeStruct(mine.shape, BF16),
        ],
        compiler_params=params(12),
        cost_estimate=cheap(),
        name="weigh",
    )(row_weight, sino, mine, low, high)


def smear(info, axial, rows):
    planes = axial.shape[1]
    detector = rows[0].shape[1]

    def body(about, ax, first_rows, own_rows, second_rows, out):
        placed = placing(about, ax).T.astype(BF16)
        odd = lax.rem(about[3], 2) == 1
        first, second = first_rows[...].astype(F32), second_rows[...].astype(F32)
        low, high = jnp.where(odd, second, first), jnp.where(odd, first, second)
        window = jnp.concatenate([low, own_rows[...], high], axis=0)
        high, low = split(window)
        out[...] = (dot(placed, high) + dot(placed, low)).astype(BF16)

    return pl.pallas_call(
        body,
        in_specs=[SM, VM, VM, VM, VM],
        out_specs=VM,
        out_shape=jax.ShapeDtypeStruct((planes, detector), BF16),
        compiler_params=params(12),
        cost_estimate=cheap(),
        name="smear",
    )(info, axial, *rows)


def pull(weights, blocks, info, places, smeared, adds=None, after=(), out_dtype=F32, joined=False):
    width, columns = weights.shape[1], weights.shape[2]
    planes = smeared.shape[0]
    tiles = weights.shape[0] // (4 * NX)
    pixels = tiles * width
    n = len(places)
    adds = adds or []
    sources = list({id(array): array for array, _ in adds}.values())
    piece = 8
    pieces = tiles // piece

    def body(blk, about, w, sm, *refs):
        given = dict(zip([id(a) for a in sources], refs[: len(sources)]))
        outs = refs[len(sources) + len(after) : -2]
        slots, sems = refs[-2:]
        origins = [base_of(about, *places[p], tiles) for p in range(n)]
        copies = [
            pltpu.make_async_copy(
                w.at[pl.ds(origins[p] + q * piece, piece)],
                slots.at[pl.ds(p * tiles + q * piece, piece)],
                sems.at[p * pieces + q],
            )
            for p in range(n)
            for q in range(pieces)
        ]
        for copy in copies:
            copy.start()
        for p in range(n):
            out, shift = (outs[0], p * pixels) if joined else (outs[p], 0)
            for q in range(pieces):
                copies[p * pieces + q].wait()
                for i in range(q * piece, (q + 1) * piece):
                    at = pl.multiple_of(blk[0, origins[p] + i] * columns, columns)
                    value = lax.dot_general(
                        sm[:, pl.ds(at, columns)],
                        slots[p * tiles + i],
                        NT,
                        preferred_element_type=F32,
                    )
                    if adds:
                        array, first = adds[p]
                        first += i * width
                        value += given[id(array)][:, first : first + width].astype(F32)
                    out[:, shift + i * width : shift + (i + 1) * width] = value.astype(out.dtype)

    shapes = [(planes, n * pixels)] if joined else [(planes, pixels)] * n
    out = pl.pallas_call(
        body,
        in_specs=[SM, SM, HBM, VM] + [VM] * len(sources) + [ANY] * len(after),
        out_specs=[VM] * len(shapes),
        out_shape=[jax.ShapeDtypeStruct(shape, out_dtype) for shape in shapes],
        scratch_shapes=[
            pltpu.VMEM((n * tiles, width, columns), BF16),
            pltpu.SemaphoreType.DMA((n * pieces,)),
        ],
        compiler_params=params(24),
        cost_estimate=cheap(),
        name="pull",
    )(blocks, info, weights, smeared, *sources, *after)
    return out[0] if joined else out


def combine(sums, size, cuts=1, after=()):
    arrays = list({id(term[0]): term[0] for terms in sums for term in terms}.values())
    half = size // 2
    planes = arrays[0].shape[0]

    def body(*refs):
        given = dict(zip([id(a) for a in arrays], refs[: len(arrays)]))
        outs = refs[len(arrays) + len(after) :]
        for s, terms in enumerate(sums):
            for h in range(2):
                value = None
                for array, first, halves in terms:
                    if h in halves:
                        first += h * half
                        more = given[id(array)][:, first : first + half].astype(F32)
                        value = more if value is None else value + more
                if cuts == 2:
                    outs[2 * s + h][...] = value.astype(BF16)
                else:
                    outs[s][:, h * half : (h + 1) * half] = value.astype(BF16)

    return pl.pallas_call(
        body,
        in_specs=[VM] * len(arrays) + [ANY] * len(after),
        out_specs=[VM] * (len(sums) * cuts),
        out_shape=[jax.ShapeDtypeStruct((planes, size // cuts), BF16)] * (len(sums) * cuts),
        compiler_params=params(16),
        cost_estimate=cheap(),
        name="combine",
    )(*arrays, *after)


def update(volume, col_weight, kept, swap, arrived):
    def body(vol, weight, mine, d, a, b, c, out):
        summed = mine[...] + d[...].astype(F32) + a[...].astype(F32) + b[...].astype(F32) + c[...].astype(F32)
        out[...] = jnp.maximum(vol[...] + weight[...] * summed, 0.0)

    planes, pixels = volume.shape
    block = pl.BlockSpec((planes, pixels // 4), lambda i: (0, i))
    return pl.pallas_call(
        body,
        grid=(4,),
        in_specs=[block] * 7,
        out_specs=block,
        out_shape=jax.ShapeDtypeStruct(volume.shape, F32),
        compiler_params=params(12),
        name="update",
    )(
        volume,
        col_weight,
        kept,
        swap,
        *arrived,
    )


def per_device(
    volume, sino, transaxial, blocks, axial, band_start, band_len, row_weight, col_weight
):
    planes, pixels = volume.shape
    rows_here = sino.shape[1]
    half = pixels // 2
    ax = jnp.swapaxes(axial[0], 0, 1)
    slab = lax.axis_index("slab")
    view = lax.axis_index("view")
    first = band_start[0, 0] - (slab - 1) * rows_here
    info = jnp.stack([view, first, band_len[0, 0], slab]).astype(jnp.int32)

    def whose(dx, dy):
        return [(dx, dy, False), (dx, dy, True)]

    own = round_volume(volume, info)
    left = send(own, UP)
    right = send(own, DOWN)
    over = send(own, ACROSS)
    swapped = send(own, CORE)
    weights = pltpu.with_memory_space_constraint(transaxial[0], pltpu.HBM)
    ahead = functools.partial(project, weights, blocks, info)
    total = ahead(whose(0, 0), [own, swapped])
    left, right, over = gate([left, right, over], total)
    far_low = send(cut(left, 0, half, total), UP)
    far_high = send(cut(right, half, half, total), DOWN)
    left_over = send(over, UP)
    right_over = send(over, DOWN)
    total = ahead(
        whose(-1, 0) + whose(1, 0), [left, send(left, CORE), right, send(right, CORE)], total
    )
    far = join(far_low, far_high, total)
    far_over = send(far, ACROSS)
    far_swapped = send(far, CORE)
    total = ahead(whose(0, 1) + [(2, 0, False)], [over, send(over, CORE), far], total)
    middle = total
    left_over, right_over = gate([left_over, right_over], total)
    total = ahead(
        [(2, 0, True)] + whose(-1, 1) + whose(1, 1),
        [far_swapped, left_over, send(left_over, CORE), right_over, send(right_over, CORE)],
        total,
    )
    (far_over,) = gate([far_over], middle)
    to_first, mine, to_second = ahead(whose(2, 1), [far_over, send(far_over, CORE)], total, ax)

    count = lax.axis_size("slab")
    first_swap, second_swap = (
        [(a, b) for i in range(start, count - 1, 2) for a, b in ((i, i + 1), (i + 1, i))]
        for start in (1, 0)
    )
    residual, own_rows, rounded = weigh(
        row_weight,
        sino,
        mine,
        lax.ppermute(to_first, "slab", first_swap),
        lax.ppermute(to_second, "slab", second_swap),
    )
    first_rows = lax.ppermute(rounded, "slab", first_swap)
    second_rows = lax.ppermute(rounded, "slab", second_swap)
    smeared = smear(info, ax, [first_rows, own_rows, second_rows])

    back = functools.partial(pull, weights, blocks, info)
    full = (0, 1)

    def others(*offsets):
        return [(dx, dy, True) for dx, dy in offsets]

    def owns(*offsets):
        return [(dx, dy, False) for dx, dy in offsets]

    def rounds(offsets, after):
        parts = back(others(*offsets), smeared, after=after, out_dtype=BF16)
        swaps = [send(part, CORE) for part in parts]
        return back(owns(*offsets), smeared, after=[parts[0]]), swaps

    def whole(array):
        return (array, 0, full)

    mine, swaps = rounds([(2, 1), (1, 1), (-1, 1)], [])
    far_sum, up_sum, down_sum = combine([[whole(a), whole(b)] for a, b in zip(mine, swaps)], pixels)
    from_over = send(far_sum, ACROSS)
    from_left = send(up_sum, UP)
    from_right = send(down_sum, DOWN)
    mine, swaps = rounds([(2, 0), (0, 1)], [far_sum])
    from_over, from_left, from_right = gate([from_over, from_left, from_right], mine[0])
    swaps = gate(swaps, from_over)
    half_up, half_down = combine([[whole(mine[0]), whole(swaps[0]), whole(from_over)]], pixels, 2)
    half_left = send(half_up, UP)
    half_right = send(half_down, DOWN)
    (over_sum,) = combine(
        [[whole(mine[1]), whole(swaps[1]), whole(from_left), whole(from_right)]],
        pixels,
        after=[half_up],
    )
    over_last = send(over_sum, ACROSS)
    mine, swaps = rounds([(1, 0), (-1, 0), (0, 0)], [over_sum])
    half_left, half_right = gate([half_left, half_right], mine[0])
    swaps = gate(swaps, half_left)
    up_sum, down_sum = combine(
        [
            [whole(mine[0]), whole(swaps[0]), (half_left, 0, (0,))],
            [whole(mine[1]), whole(swaps[1]), (half_right, -half, (1,))],
        ],
        pixels,
    )
    left_last = send(up_sum, UP)
    right_last = send(down_sum, DOWN)
    updated = update(
        volume, col_weight, mine[2], swaps[2], [over_last, left_last, right_last]
    )
    return updated, residual[None]


def solution(mesh):
    in_specs = (
        P("slab", "view"),
        P("view", "slab", None),
        P("view", None, None, None),
        P("view", None),
        P("view", "slab", None),
        P("view", "slab"),
        P("view", "slab"),
        P("view", "slab", None),
        P("slab", "view"),
    )
    out_specs = (P("slab", "view"), P("view", "slab", None))
    return jax.shard_map(
        per_device, mesh=mesh, in_specs=in_specs, out_specs=out_specs, check_vma=False
    )
```

```python
import functools
import jax
import jax.numpy as jnp
from jax import lax
from jax.experimental import pallas as pl
from jax.experimental.pallas import tpu as pltpu
from jax.sharding import PartitionSpec as P

F32 = jnp.float32
BF16 = jnp.bfloat16
MIB = 2**20
VM = pl.BlockSpec(memory_space=pltpu.VMEM)
SM = pl.BlockSpec(memory_space=pltpu.SMEM)
ANY = pl.BlockSpec(memory_space=pl.ANY)
HBM = pl.BlockSpec(memory_space=pltpu.HBM)
NT = (((1,), (1,)), ((), ()))
NX = 4


def place(y, x, c):
    return (y % 2) * 2 * NX + (x % NX) * 2 + c


def moves(step):
    return [
        (place(y, x, c), place(*step(y, x, c)))
        for y in range(2)
        for x in range(NX)
        for c in range(2)
    ]


UP = moves(lambda y, x, c: (y, x + 1, c))
DOWN = moves(lambda y, x, c: (y, x - 1, c))
ACROSS = moves(lambda y, x, c: (y + 1, x, c))
CORE = moves(lambda y, x, c: (y, x, 1 - c))


def send(array, pairs):
    return lax.ppermute(array, "view", pairs)


def params(mib):
    return pltpu.CompilerParams(vmem_limit_bytes=mib * MIB)


def split(value):
    high = value.astype(BF16)
    return high, (value - high.astype(F32)).astype(BF16)


def dot(a, b):
    return jnp.dot(a, b, preferred_element_type=F32)


def base_of(info, dx, dy, other, tiles):
    view = info[0]
    y, x, c = view // (2 * NX), (view // 2) % NX, view % 2
    c = 1 - c if other else c
    owner = lax.rem(y + dy, 2) * 2 * NX + lax.rem(x + dx + NX, NX) * 2 + c
    return owner * tiles


def cheap():
    return pl.CostEstimate(flops=1, bytes_accessed=1, transcendentals=0)


def round_volume(volume, info):
    def body(source, about, out):
        out[...] = source[...].astype(BF16)

    return pl.pallas_call(
        body,
        in_specs=[VM, SM],
        out_specs=VM,
        out_shape=jax.ShapeDtypeStruct(volume.shape, BF16),
        compiler_params=params(12),
        cost_estimate=cheap(),
        name="round_volume",
    )(volume, info)


def gate(arrays, after):
    n = len(arrays)

    def body(*refs):
        pass

    return pl.pallas_call(
        body,
        in_specs=[ANY] * (n + 1),
        out_specs=[ANY] * n,
        out_shape=[jax.ShapeDtypeStruct(a.shape, a.dtype) for a in arrays],
        input_output_aliases={i: i for i in range(n)},
        compiler_params=params(12),
        cost_estimate=cheap(),
        name="gate",
    )(*arrays, after)


def cut(array, start, size, after):
    def body(source, earlier, out):
        out[...] = source[:, start : start + size]

    return pl.pallas_call(
        body,
        in_specs=[VM, ANY],
        out_specs=VM,
        out_shape=jax.ShapeDtypeStruct((array.shape[0], size), array.dtype),
        compiler_params=params(12),
        cost_estimate=cheap(),
        name="cut",
    )(array, after)


def join(low, high, after):
    size = low.shape[1]

    def body(a, b, earlier, out):
        out[:, :size] = a[...]
        out[:, size:] = b[...]

    return pl.pallas_call(
        body,
        in_specs=[VM, VM, ANY],
        out_specs=VM,
        out_shape=jax.ShapeDtypeStruct((low.shape[0], 2 * size), low.dtype),
        compiler_params=params(12),
        cost_estimate=cheap(),
        name="join",
    )(low, high, after)


def load_footprints(source, after):
    pieces = 16
    each = source.shape[0] // pieces

    def body(src, earlier, target, sems):
        copies = [
            pltpu.make_async_copy(
                src.at[pl.ds(i * each, each)], target.at[pl.ds(i * each, each)], sems.at[i]
            )
            for i in range(pieces)
        ]
        for copy in copies:
            copy.start()
        for copy in copies:
            copy.wait()

    return pl.pallas_call(
        body,
        in_specs=[HBM, ANY],
        out_specs=VM,
        out_shape=pltpu.VMEM(source.shape, source.dtype),
        scratch_shapes=[pltpu.SemaphoreType.DMA((pieces,))],
        compiler_params=params(12),
        cost_estimate=pl.CostEstimate(flops=1, bytes_accessed=source.size * 2, transcendentals=0),
        name="load_footprints",
    )(source, after)


def placing(info, axial):
    most, planes = axial.shape
    window = 48
    first, length = info[1], info[2]
    live = lax.broadcasted_iota(jnp.int32, (most, planes), 0) < length
    masked = jnp.where(live, axial[...].astype(F32), 0.0).astype(BF16)
    hot = (
        lax.broadcasted_iota(jnp.int32, (window, most), 1) + first
        == lax.broadcasted_iota(jnp.int32, (window, most), 0)
    )
    return dot(jnp.where(hot, 1.0, 0.0).astype(BF16), masked)


def project(weights, blocks, info, places, shards, total=None, axial=None):
    planes, pixels = shards[0].shape
    width, columns = weights.shape[1], weights.shape[2]
    tiles = pixels // width
    detector = 8 * columns
    n = len(shards)
    started = total is not None
    last = axial is not None
    piece = 4
    pieces = tiles // piece

    def body(blk, about, w, *refs):
        refs = list(refs)
        parts = [refs.pop(0) for _ in range(n)]
        before = refs.pop(0) if started else None
        ax = refs.pop(0) if last else None
        outs = [refs.pop(0) for _ in range(3)] if last else None
        acc, slots, sems = refs
        origins = [base_of(about, *places[p], tiles) for p in range(n)]
        copies = [
            pltpu.make_async_copy(
                w.at[pl.ds(origins[p] + q * piece, piece)],
                slots.at[pl.ds(p * tiles + q * piece, piece)],
                sems.at[p * pieces + q],
            )
            for p in range(n)
            for q in range(pieces)
        ]
        for copy in copies:
            copy.start()
        acc[...] = before[...] if started else jnp.zeros(acc.shape, F32)
        for p in range(n):
            for q in range(pieces):
                copies[p * pieces + q].wait()
                for i in range(q * piece, (q + 1) * piece):
                    at = pl.multiple_of(blk[0, origins[p] + i] * columns, columns)
                    row = parts[p][:, i * width : (i + 1) * width]
                    acc[:, pl.ds(at, columns)] += dot(row, slots[p * tiles + i])
        if last:
            placed = placing(about, ax).astype(BF16)
            high, low = split(acc[...])
            spread = dot(placed, high) + dot(placed, low)
            outs[1][...] = spread[16:32]
            odd = lax.rem(about[3], 2)

            @pl.when(odd == 1)
            def _():
                outs[0][...] = spread[32:]
                outs[2][...] = spread[:16]

            @pl.when(odd == 0)
            def _():
                outs[0][...] = spread[:16]
                outs[2][...] = spread[32:]

    args = [blocks, info, weights, *shards]
    specs = [SM, SM, HBM] + [VM] * n
    if started:
        args.append(total)
        specs.append(VM)
    scratch = [
        pltpu.VMEM((n * tiles, width, columns), BF16),
        pltpu.SemaphoreType.DMA((n * pieces,)),
    ]
    if last:
        args.append(axial)
        specs.append(VM)
        out_shape = [jax.ShapeDtypeStruct((16, detector), F32)] * 3
        out_specs = [VM] * 3
        scratch = [pltpu.VMEM((planes, detector), F32)] + scratch
    else:
        out_shape = jax.ShapeDtypeStruct((planes, detector), F32)
        out_specs = VM
    return pl.pallas_call(
        body,
        in_specs=specs,
        out_specs=out_specs,
        out_shape=out_shape,
        scratch_shapes=scratch,
        compiler_params=params(2 * n + 4),
        cost_estimate=cheap(),
        name="project",
    )(*args)


def weigh(row_weight, sino, mine, low, high):
    def body(rw, measured, a, b, c, out, again, short):
        value = rw[0] * (measured[0] - (a[...] + b[...] + c[...]))
        out[...] = value
        again[...] = value
        short[...] = value.astype(BF16)

    return pl.pallas_call(
        body,
        in_specs=[VM] * 5,
        out_specs=[VM] * 3,
        out_shape=[jax.ShapeDtypeStruct(mine.shape, F32)] * 2
        + [
            jax.ShapeDtypeStruct(mine.shape, BF16),
        ],
        compiler_params=params(12),
        cost_estimate=cheap(),
        name="weigh",
    )(row_weight, sino, mine, low, high)


def smear(about, ax, rows, out):
    placed = placing(about, ax).T.astype(BF16)
    odd = lax.rem(about[3], 2) == 1
    first, second = rows[0][...].astype(F32), rows[2][...].astype(F32)
    low, high = jnp.where(odd, second, first), jnp.where(odd, first, second)
    high, low = split(jnp.concatenate([low, rows[1][...], high], axis=0))
    out[...] = (dot(placed, high) + dot(placed, low)).astype(BF16)


def pull(weights, blocks, info, places, smeared, after=(), out_dtype=F32, bands=None):
    width, columns = weights.shape[1], weights.shape[2]
    own = bands is not None
    given = list(bands) if own else [smeared]
    planes = bands[0].shape[1] if own else smeared.shape[0]
    tiles = weights.shape[0] // (4 * NX)
    pixels = tiles * width
    n = len(places)
    piece = 8
    pieces = tiles // piece

    def body(blk, about, w, *refs):
        args = refs[: len(given)]
        outs = refs[len(given) + len(after) : -2]
        slots, sems = refs[-2:]
        origins = [base_of(about, *places[p], tiles) for p in range(n)]
        copies = [
            pltpu.make_async_copy(
                w.at[pl.ds(origins[p] + q * piece, piece)],
                slots.at[pl.ds(p * tiles + q * piece, piece)],
                sems.at[p * pieces + q],
            )
            for p in range(n)
            for q in range(pieces)
        ]
        for copy in copies:
            copy.start()
        if own:
            sm = outs[n]
            smear(about, args[0], args[1:], sm)
        else:
            sm = args[0]
        for p in range(n):
            for q in range(pieces):
                copies[p * pieces + q].wait()
                for i in range(q * piece, (q + 1) * piece):
                    at = pl.multiple_of(blk[0, origins[p] + i] * columns, columns)
                    value = lax.dot_general(
                        sm[:, pl.ds(at, columns)],
                        slots[p * tiles + i],
                        NT,
                        preferred_element_type=F32,
                    )
                    outs[p][:, i * width : (i + 1) * width] = value.astype(out_dtype)

    out_shape = [jax.ShapeDtypeStruct((planes, pixels), out_dtype)] * n
    if own:
        out_shape.append(jax.ShapeDtypeStruct((planes, bands[1].shape[1]), BF16))
    return pl.pallas_call(
        body,
        in_specs=[SM, SM, HBM] + [VM] * len(given) + [ANY] * len(after),
        out_specs=[VM] * len(out_shape),
        out_shape=out_shape,
        scratch_shapes=[
            pltpu.VMEM((n * tiles, width, columns), BF16),
            pltpu.SemaphoreType.DMA((n * pieces,)),
        ],
        compiler_params=params(24),
        cost_estimate=cheap(),
        name="pull",
    )(blocks, info, weights, *given, *after)


def combine(sums, size, cuts=1, after=()):
    arrays = list({id(term[0]): term[0] for terms in sums for term in terms}.values())
    half = size // 2
    planes = arrays[0].shape[0]

    def body(*refs):
        given = dict(zip([id(a) for a in arrays], refs[: len(arrays)]))
        outs = refs[len(arrays) + len(after) :]
        for s, terms in enumerate(sums):
            for h in range(2):
                value = None
                for array, first, halves in terms:
                    if h in halves:
                        first += h * half
                        more = given[id(array)][:, first : first + half].astype(F32)
                        value = more if value is None else value + more
                if cuts == 2:
                    outs[2 * s + h][...] = value.astype(BF16)
                else:
                    outs[s][:, h * half : (h + 1) * half] = value.astype(BF16)

    return pl.pallas_call(
        body,
        in_specs=[VM] * len(arrays) + [ANY] * len(after),
        out_specs=[VM] * (len(sums) * cuts),
        out_shape=[jax.ShapeDtypeStruct((planes, size // cuts), BF16)] * (len(sums) * cuts),
        compiler_params=params(16),
        cost_estimate=cheap(),
        name="combine",
    )(*arrays, *after)


def update(volume, col_weight, kept, swap, arrived):
    def body(vol, weight, mine, d, a, b, c, out):
        summed = mine[...] + d[...].astype(F32) + a[...].astype(F32) + b[...].astype(F32) + c[...].astype(F32)
        out[...] = jnp.maximum(vol[...] + weight[...] * summed, 0.0)

    planes, pixels = volume.shape
    block = pl.BlockSpec((planes, pixels // 4), lambda i: (0, i))
    return pl.pallas_call(
        body,
        grid=(4,),
        in_specs=[block] * 7,
        out_specs=block,
        out_shape=jax.ShapeDtypeStruct(volume.shape, F32),
        compiler_params=params(12),
        name="update",
    )(
        volume,
        col_weight,
        kept,
        swap,
        *arrived,
    )


def per_device(
    volume, sino, transaxial, blocks, axial, band_start, band_len, row_weight, col_weight
):
    planes, pixels = volume.shape
    rows_here = sino.shape[1]
    half = pixels // 2
    ax = jnp.swapaxes(axial[0], 0, 1)
    slab = lax.axis_index("slab")
    view = lax.axis_index("view")
    first = band_start[0, 0] - (slab - 1) * rows_here
    info = jnp.stack([view, first, band_len[0, 0], slab]).astype(jnp.int32)

    def whose(dx, dy):
        return [(dx, dy, False), (dx, dy, True)]

    own = round_volume(volume, info)
    left = send(own, UP)
    right = send(own, DOWN)
    over = send(own, ACROSS)
    swapped = send(own, CORE)
    weights = pltpu.with_memory_space_constraint(transaxial[0], pltpu.HBM)
    ahead = functools.partial(project, weights, blocks, info)
    total = ahead(whose(0, 0), [own, swapped])
    left, right = gate([left, right], total)
    (over,) = gate([over], left)
    far_low = send(cut(left, 0, half, total), UP)
    far_high = send(cut(right, half, half, total), DOWN)
    left_over = send(over, UP)
    right_over = send(over, DOWN)
    total = ahead(
        whose(-1, 0) + whose(1, 0), [left, send(left, CORE), right, send(right, CORE)], total
    )
    far = join(far_low, far_high, total)
    far_over = send(far, ACROSS)
    far_swapped = send(far, CORE)
    total = ahead(whose(0, 1) + [(2, 0, False)], [over, send(over, CORE), far], total)
    middle = total
    left_over, right_over = gate([left_over, right_over], total)
    total = ahead(
        [(2, 0, True)] + whose(-1, 1) + whose(1, 1),
        [far_swapped, left_over, send(left_over, CORE), right_over, send(right_over, CORE)],
        total,
    )
    (far_over,) = gate([far_over], middle)
    to_first, mine, to_second = ahead(whose(2, 1), [far_over, send(far_over, CORE)], total, ax)

    count = lax.axis_size("slab")
    first_swap, second_swap = (
        [(a, b) for i in range(start, count - 1, 2) for a, b in ((i, i + 1), (i + 1, i))]
        for start in (1, 0)
    )
    residual, own_rows, rounded = weigh(
        row_weight,
        sino,
        mine,
        lax.ppermute(to_first, "slab", first_swap),
        lax.ppermute(to_second, "slab", second_swap),
    )
    first_rows = lax.ppermute(rounded, "slab", first_swap)
    second_rows = lax.ppermute(rounded, "slab", second_swap)

    back = functools.partial(pull, weights, blocks, info)
    full = (0, 1)

    def others(*offsets):
        return [(dx, dy, True) for dx, dy in offsets]

    def owns(*offsets):
        return [(dx, dy, False) for dx, dy in offsets]

    def swap_parts(offsets, after):
        parts = back(others(*offsets), smeared, after=after, out_dtype=BF16)
        return parts[0], [send(part, CORE) for part in parts]

    def whole(array):
        return (array, 0, full)

    offsets = [(2, 1), (1, 1), (-1, 1)]
    *parts, smeared = back(
        others(*offsets), None, out_dtype=BF16, bands=[ax, first_rows, own_rows, second_rows]
    )
    swaps = [send(part, CORE) for part in parts]
    part = parts[0]
    mine = back(owns(*offsets), smeared, after=[part])
    far_sum, up_sum, down_sum = combine([[whole(a), whole(b)] for a, b in zip(mine, swaps)], pixels)
    from_over = send(far_sum, ACROSS)
    from_left = send(up_sum, UP)
    from_right = send(down_sum, DOWN)
    offsets = [(2, 0), (0, 1)]
    part, swaps = swap_parts(offsets, [far_sum])
    mine = back(owns(*offsets), smeared, after=[part])
    offsets = [(1, 0), (-1, 0), (0, 0)]
    part, last_swaps = swap_parts(offsets, [mine[0]])
    from_over, from_left, from_right = gate([from_over, from_left, from_right], part)
    swaps = gate(swaps, from_over)
    half_up, half_down = combine([[whole(mine[0]), whole(swaps[0]), whole(from_over)]], pixels, 2)
    half_left = send(half_up, UP)
    half_right = send(half_down, DOWN)
    (over_sum,) = combine(
        [[whole(mine[1]), whole(swaps[1]), whole(from_left), whole(from_right)]],
        pixels,
        after=[half_up],
    )
    over_last = send(over_sum, ACROSS)
    mine = back(owns(*offsets), smeared, after=[over_sum])
    half_left, half_right = gate([half_left, half_right], mine[0])
    swaps = gate(last_swaps, half_left)
    up_sum, down_sum = combine(
        [
            [whole(mine[0]), whole(swaps[0]), (half_left, 0, (0,))],
            [whole(mine[1]), whole(swaps[1]), (half_right, -half, (1,))],
        ],
        pixels,
    )
    left_last = send(up_sum, UP)
    right_last = send(down_sum, DOWN)
    updated = update(
        volume, col_weight, mine[2], swaps[2], [over_last, left_last, right_last]
    )
    return updated, residual[None]


def solution(mesh):
    in_specs = (
        P("slab", "view"),
        P("view", "slab", None),
        P("view", None, None, None),
        P("view", None),
        P("view", "slab", None),
        P("view", "slab"),
        P("view", "slab"),
        P("view", "slab", None),
        P("slab", "view"),
    )
    out_specs = (P("slab", "view"), P("view", "slab", None))
    return jax.shard_map(
        per_device, mesh=mesh, in_specs=in_specs, out_specs=out_specs, check_vma=False
    )
```

```python
import functools
import jax
import jax.numpy as jnp
from jax import lax
from jax.experimental import pallas as pl
from jax.experimental.pallas import tpu as pltpu
from jax.sharding import PartitionSpec as P

F32 = jnp.float32
BF16 = jnp.bfloat16
MIB = 2**20
VM = pl.BlockSpec(memory_space=pltpu.VMEM)
SM = pl.BlockSpec(memory_space=pltpu.SMEM)
ANY = pl.BlockSpec(memory_space=pl.ANY)
HBM = pl.BlockSpec(memory_space=pltpu.HBM)
NT = (((1,), (1,)), ((), ()))
NX = 4


def place(y, x, c):
    return (y % 2) * 2 * NX + (x % NX) * 2 + c


def moves(step):
    return [
        (place(y, x, c), place(*step(y, x, c)))
        for y in range(2)
        for x in range(NX)
        for c in range(2)
    ]


UP = moves(lambda y, x, c: (y, x + 1, c))
DOWN = moves(lambda y, x, c: (y, x - 1, c))
ACROSS = moves(lambda y, x, c: (y + 1, x, c))
CORE = moves(lambda y, x, c: (y, x, 1 - c))


def send(array, pairs):
    return lax.ppermute(array, "view", pairs)


def params(mib):
    return pltpu.CompilerParams(vmem_limit_bytes=mib * MIB)


def split(value):
    high = value.astype(BF16)
    return high, (value - high.astype(F32)).astype(BF16)


def dot(a, b):
    return jnp.dot(a, b, preferred_element_type=F32)


def base_of(info, dx, dy, other, tiles):
    view = info[0]
    y, x, c = view // (2 * NX), (view // 2) % NX, view % 2
    c = 1 - c if other else c
    owner = lax.rem(y + dy, 2) * 2 * NX + lax.rem(x + dx + NX, NX) * 2 + c
    return owner * tiles


def cheap():
    return pl.CostEstimate(flops=1, bytes_accessed=1, transcendentals=0)


def round_volume(volume, info):
    def body(source, about, out):
        out[...] = source[...].astype(BF16)

    return pl.pallas_call(
        body,
        in_specs=[VM, SM],
        out_specs=VM,
        out_shape=jax.ShapeDtypeStruct(volume.shape, BF16),
        compiler_params=params(12),
        cost_estimate=cheap(),
        name="round_volume",
    )(volume, info)


def gate(arrays, after):
    n = len(arrays)

    def body(*refs):
        pass

    return pl.pallas_call(
        body,
        in_specs=[ANY] * (n + 1),
        out_specs=[ANY] * n,
        out_shape=[jax.ShapeDtypeStruct(a.shape, a.dtype) for a in arrays],
        input_output_aliases={i: i for i in range(n)},
        compiler_params=params(12),
        cost_estimate=cheap(),
        name="gate",
    )(*arrays, after)


def cut(array, start, size, after):
    def body(source, earlier, out):
        out[...] = source[:, start : start + size]

    return pl.pallas_call(
        body,
        in_specs=[VM, ANY],
        out_specs=VM,
        out_shape=jax.ShapeDtypeStruct((array.shape[0], size), array.dtype),
        compiler_params=params(12),
        cost_estimate=cheap(),
        name="cut",
    )(array, after)


def join(low, high, after):
    size = low.shape[1]

    def body(a, b, earlier, out):
        out[:, :size] = a[...]
        out[:, size:] = b[...]

    return pl.pallas_call(
        body,
        in_specs=[VM, VM, ANY],
        out_specs=VM,
        out_shape=jax.ShapeDtypeStruct((low.shape[0], 2 * size), low.dtype),
        compiler_params=params(12),
        cost_estimate=cheap(),
        name="join",
    )(low, high, after)


def load_footprints(source, after):
    pieces = 16
    each = source.shape[0] // pieces

    def body(src, earlier, target, sems):
        copies = [
            pltpu.make_async_copy(
                src.at[pl.ds(i * each, each)], target.at[pl.ds(i * each, each)], sems.at[i]
            )
            for i in range(pieces)
        ]
        for copy in copies:
            copy.start()
        for copy in copies:
            copy.wait()

    return pl.pallas_call(
        body,
        in_specs=[HBM, ANY],
        out_specs=VM,
        out_shape=pltpu.VMEM(source.shape, source.dtype),
        scratch_shapes=[pltpu.SemaphoreType.DMA((pieces,))],
        compiler_params=params(12),
        cost_estimate=pl.CostEstimate(flops=1, bytes_accessed=source.size * 2, transcendentals=0),
        name="load_footprints",
    )(source, after)


def placing(info, axial):
    most, planes = axial.shape
    window = 48
    first, length = info[1], info[2]
    live = lax.broadcasted_iota(jnp.int32, (most, planes), 0) < length
    masked = jnp.where(live, axial[...].astype(F32), 0.0).astype(BF16)
    hot = (
        lax.broadcasted_iota(jnp.int32, (window, most), 1) + first
        == lax.broadcasted_iota(jnp.int32, (window, most), 0)
    )
    return dot(jnp.where(hot, 1.0, 0.0).astype(BF16), masked)


def project(weights, blocks, info, places, shards, total=None, axial=None):
    planes, pixels = shards[0].shape
    width, columns = weights.shape[1], weights.shape[2]
    tiles = pixels // width
    detector = 8 * columns
    n = len(shards)
    started = total is not None
    last = axial is not None
    piece = 8
    pieces = tiles // piece

    def body(blk, about, w, *refs):
        refs = list(refs)
        parts = [refs.pop(0) for _ in range(n)]
        before = refs.pop(0) if started else None
        ax = refs.pop(0) if last else None
        outs = [refs.pop(0) for _ in range(3)] if last else None
        acc, slots, sems = refs
        origins = [base_of(about, *places[p], tiles) for p in range(n)]
        copies = [
            pltpu.make_async_copy(
                w.at[pl.ds(origins[p] + q * piece, piece)],
                slots.at[pl.ds(p * tiles + q * piece, piece)],
                sems.at[p * pieces + q],
            )
            for p in range(n)
            for q in range(pieces)
        ]
        for copy in copies:
            copy.start()
        acc[...] = before[...] if started else jnp.zeros(acc.shape, F32)
        for p in range(n):
            for q in range(pieces):
                copies[p * pieces + q].wait()
                for i in range(q * piece, (q + 1) * piece):
                    at = pl.multiple_of(blk[0, origins[p] + i] * columns, columns)
                    row = parts[p][:, i * width : (i + 1) * width]
                    acc[:, pl.ds(at, columns)] += dot(row, slots[p * tiles + i])
        if last:
            placed = placing(about, ax).astype(BF16)
            high, low = split(acc[...])
            spread = dot(placed, high) + dot(placed, low)
            outs[1][...] = spread[16:32]
            odd = lax.rem(about[3], 2)

            @pl.when(odd == 1)
            def _():
                outs[0][...] = spread[32:]
                outs[2][...] = spread[:16]

            @pl.when(odd == 0)
            def _():
                outs[0][...] = spread[:16]
                outs[2][...] = spread[32:]

    args = [blocks, info, weights, *shards]
    specs = [SM, SM, HBM] + [VM] * n
    if started:
        args.append(total)
        specs.append(VM)
    scratch = [
        pltpu.VMEM((n * tiles, width, columns), BF16),
        pltpu.SemaphoreType.DMA((n * pieces,)),
    ]
    if last:
        args.append(axial)
        specs.append(VM)
        out_shape = [jax.ShapeDtypeStruct((16, detector), F32)] * 3
        out_specs = [VM] * 3
        scratch = [pltpu.VMEM((planes, detector), F32)] + scratch
    else:
        out_shape = jax.ShapeDtypeStruct((planes, detector), F32)
        out_specs = VM
    return pl.pallas_call(
        body,
        in_specs=specs,
        out_specs=out_specs,
        out_shape=out_shape,
        scratch_shapes=scratch,
        compiler_params=params(2 * n + 4),
        cost_estimate=cheap(),
        name="project",
    )(*args)


def weigh(row_weight, sino, mine, low, high):
    def body(rw, measured, a, b, c, out, again, short):
        value = rw[0] * (measured[0] - (a[...] + b[...] + c[...]))
        out[...] = value
        again[...] = value
        short[...] = value.astype(BF16)

    return pl.pallas_call(
        body,
        in_specs=[VM] * 5,
        out_specs=[VM] * 3,
        out_shape=[jax.ShapeDtypeStruct(mine.shape, F32)] * 2
        + [
            jax.ShapeDtypeStruct(mine.shape, BF16),
        ],
        compiler_params=params(12),
        cost_estimate=cheap(),
        name="weigh",
    )(row_weight, sino, mine, low, high)


def smear(about, ax, rows, out):
    placed = placing(about, ax).T.astype(BF16)
    odd = lax.rem(about[3], 2) == 1
    first, second = rows[0][...].astype(F32), rows[2][...].astype(F32)
    low, high = jnp.where(odd, second, first), jnp.where(odd, first, second)
    high, low = split(jnp.concatenate([low, rows[1][...], high], axis=0))
    out[...] = (dot(placed, high) + dot(placed, low)).astype(BF16)


def pull(weights, blocks, info, places, smeared, after=(), out_dtype=F32, bands=None):
    width, columns = weights.shape[1], weights.shape[2]
    own = bands is not None
    given = list(bands) if own else [smeared]
    planes = bands[0].shape[1] if own else smeared.shape[0]
    tiles = weights.shape[0] // (4 * NX)
    pixels = tiles * width
    n = len(places)
    piece = 8
    pieces = tiles // piece

    def body(blk, about, w, *refs):
        args = refs[: len(given)]
        outs = refs[len(given) + len(after) : -2]
        slots, sems = refs[-2:]
        origins = [base_of(about, *places[p], tiles) for p in range(n)]
        copies = [
            pltpu.make_async_copy(
                w.at[pl.ds(origins[p] + q * piece, piece)],
                slots.at[pl.ds(p * tiles + q * piece, piece)],
                sems.at[p * pieces + q],
            )
            for p in range(n)
            for q in range(pieces)
        ]
        for copy in copies:
            copy.start()
        if own:
            sm = outs[n]
            smear(about, args[0], args[1:], sm)
        else:
            sm = args[0]
        for p in range(n):
            for q in range(pieces):
                copies[p * pieces + q].wait()
                for i in range(q * piece, (q + 1) * piece):
                    at = pl.multiple_of(blk[0, origins[p] + i] * columns, columns)
                    value = lax.dot_general(
                        sm[:, pl.ds(at, columns)],
                        slots[p * tiles + i],
                        NT,
                        preferred_element_type=F32,
                    )
                    outs[p][:, i * width : (i + 1) * width] = value.astype(out_dtype)

    out_shape = [jax.ShapeDtypeStruct((planes, pixels), out_dtype)] * n
    if own:
        out_shape.append(jax.ShapeDtypeStruct((planes, bands[1].shape[1]), BF16))
    return pl.pallas_call(
        body,
        in_specs=[SM, SM, HBM] + [VM] * len(given) + [ANY] * len(after),
        out_specs=[VM] * len(out_shape),
        out_shape=out_shape,
        scratch_shapes=[
            pltpu.VMEM((n * tiles, width, columns), BF16),
            pltpu.SemaphoreType.DMA((n * pieces,)),
        ],
        compiler_params=params(24),
        cost_estimate=cheap(),
        name="pull",
    )(blocks, info, weights, *given, *after)


def combine(sums, size, cuts=1, after=()):
    arrays = list({id(term[0]): term[0] for terms in sums for term in terms}.values())
    half = size // 2
    planes = arrays[0].shape[0]

    def body(*refs):
        given = dict(zip([id(a) for a in arrays], refs[: len(arrays)]))
        outs = refs[len(arrays) + len(after) :]
        for s, terms in enumerate(sums):
            for h in range(2):
                value = None
                for array, first, halves in terms:
                    if h in halves:
                        first += h * half
                        more = given[id(array)][:, first : first + half].astype(F32)
                        value = more if value is None else value + more
                if cuts == 2:
                    outs[2 * s + h][...] = value.astype(BF16)
                else:
                    outs[s][:, h * half : (h + 1) * half] = value.astype(BF16)

    return pl.pallas_call(
        body,
        in_specs=[VM] * len(arrays) + [ANY] * len(after),
        out_specs=[VM] * (len(sums) * cuts),
        out_shape=[jax.ShapeDtypeStruct((planes, size // cuts), BF16)] * (len(sums) * cuts),
        compiler_params=params(16),
        cost_estimate=cheap(),
        name="combine",
    )(*arrays, *after)


def update(volume, col_weight, kept, swap, arrived):
    def body(vol, weight, mine, d, a, b, c, out):
        summed = mine[...] + d[...].astype(F32) + a[...].astype(F32) + b[...].astype(F32) + c[...].astype(F32)
        out[...] = jnp.maximum(vol[...] + weight[...] * summed, 0.0)

    planes, pixels = volume.shape
    block = pl.BlockSpec((planes, pixels // 2), lambda i: (0, i))
    return pl.pallas_call(
        body,
        grid=(2,),
        in_specs=[block] * 7,
        out_specs=block,
        out_shape=jax.ShapeDtypeStruct(volume.shape, F32),
        compiler_params=params(12),
        name="update",
    )(
        volume,
        col_weight,
        kept,
        swap,
        *arrived,
    )


def per_device(
    volume, sino, transaxial, blocks, axial, band_start, band_len, row_weight, col_weight
):
    planes, pixels = volume.shape
    rows_here = sino.shape[1]
    half = pixels // 2
    ax = jnp.swapaxes(axial[0], 0, 1)
    slab = lax.axis_index("slab")
    view = lax.axis_index("view")
    first = band_start[0, 0] - (slab - 1) * rows_here
    info = jnp.stack([view, first, band_len[0, 0], slab]).astype(jnp.int32)

    def whose(dx, dy):
        return [(dx, dy, False), (dx, dy, True)]

    own = round_volume(volume, info)
    left = send(own, UP)
    right = send(own, DOWN)
    over = send(own, ACROSS)
    swapped = send(own, CORE)
    weights = pltpu.with_memory_space_constraint(transaxial[0], pltpu.HBM)
    ahead = functools.partial(project, weights, blocks, info)
    total = ahead(whose(0, 0), [own, swapped])
    left, right = gate([left, right], total)
    (over,) = gate([over], left)
    far_low = send(cut(left, 0, half, total), UP)
    far_high = send(cut(right, half, half, total), DOWN)
    left_over = send(over, UP)
    right_over = send(over, DOWN)
    total = ahead(
        whose(-1, 0) + whose(1, 0), [left, send(left, CORE), right, send(right, CORE)], total
    )
    far = join(far_low, far_high, total)
    far_over = send(far, ACROSS)
    far_swapped = send(far, CORE)
    total = ahead(whose(0, 1) + [(2, 0, False)], [over, send(over, CORE), far], total)
    left_over, right_over = gate([left_over, right_over], total)
    total = ahead(
        [(2, 0, True), (-1, 1, False), (1, 1, False)],
        [far_swapped, left_over, right_over],
        total,
    )
    left_swapped, right_swapped = send(left_over, CORE), send(right_over, CORE)
    (far_over,) = gate([far_over], total)
    to_first, mine, to_second = ahead(
        [(-1, 1, True), (1, 1, True)] + whose(2, 1),
        [left_swapped, right_swapped, far_over, send(far_over, CORE)],
        total,
        ax,
    )

    count = lax.axis_size("slab")
    first_swap, second_swap = (
        [(a, b) for i in range(start, count - 1, 2) for a, b in ((i, i + 1), (i + 1, i))]
        for start in (1, 0)
    )
    residual, own_rows, rounded = weigh(
        row_weight,
        sino,
        mine,
        lax.ppermute(to_first, "slab", first_swap),
        lax.ppermute(to_second, "slab", second_swap),
    )
    first_rows = lax.ppermute(rounded, "slab", first_swap)
    second_rows = lax.ppermute(rounded, "slab", second_swap)

    back = functools.partial(pull, weights, blocks, info)
    full = (0, 1)

    def others(*offsets):
        return [(dx, dy, True) for dx, dy in offsets]

    def owns(*offsets):
        return [(dx, dy, False) for dx, dy in offsets]

    def swap_parts(offsets, after):
        parts = back(others(*offsets), smeared, after=after, out_dtype=BF16)
        return parts[0], [send(part, CORE) for part in parts]

    def whole(array):
        return (array, 0, full)

    offsets = [(2, 1), (1, 1), (-1, 1)]
    *parts, smeared = back(
        others(*offsets), None, out_dtype=BF16, bands=[ax, first_rows, own_rows, second_rows]
    )
    swaps = [send(part, CORE) for part in parts]
    part = parts[0]
    mine = back(owns(*offsets), smeared, after=[part])
    far_sum, up_sum, down_sum = combine([[whole(a), whole(b)] for a, b in zip(mine, swaps)], pixels)
    from_over = send(far_sum, ACROSS)
    from_left = send(up_sum, UP)
    from_right = send(down_sum, DOWN)
    offsets = [(2, 0), (0, 1)]
    part, swaps = swap_parts(offsets, [far_sum])
    mine = back(owns(*offsets), smeared, after=[part])
    offsets = [(1, 0), (-1, 0), (0, 0)]
    part, last_swaps = swap_parts(offsets, [mine[0]])
    from_over, from_left, from_right = gate([from_over, from_left, from_right], part)
    swaps = gate(swaps, from_over)
    half_up, half_down = combine([[whole(mine[0]), whole(swaps[0]), whole(from_over)]], pixels, 2)
    half_left = send(half_up, UP)
    half_right = send(half_down, DOWN)
    (over_sum,) = combine(
        [[whole(mine[1]), whole(swaps[1]), whole(from_left), whole(from_right)]],
        pixels,
        after=[half_up],
    )
    over_last = send(over_sum, ACROSS)
    mine = back(owns(*offsets), smeared, after=[over_sum])
    half_left, half_right = gate([half_left, half_right], mine[0])
    swaps = gate(last_swaps, half_left)
    up_sum, down_sum = combine(
        [
            [whole(mine[0]), whole(swaps[0]), (half_left, 0, (0,))],
            [whole(mine[1]), whole(swaps[1]), (half_right, -half, (1,))],
        ],
        pixels,
    )
    left_last = send(up_sum, UP)
    right_last = send(down_sum, DOWN)
    updated = update(
        volume, col_weight, mine[2], swaps[2], [over_last, left_last, right_last]
    )
    return updated, residual[None]


def solution(mesh):
    in_specs = (
        P("slab", "view"),
        P("view", "slab", None),
        P("view", None, None, None),
        P("view", None),
        P("view", "slab", None),
        P("view", "slab"),
        P("view", "slab"),
        P("view", "slab", None),
        P("slab", "view"),
    )
    out_specs = (P("slab", "view"), P("view", "slab", None))
    return jax.shard_map(
        per_device, mesh=mesh, in_specs=in_specs, out_specs=out_specs, check_vma=False
    )
```

```python
import functools
import jax
import jax.numpy as jnp
from jax import lax
from jax.experimental import pallas as pl
from jax.experimental.pallas import tpu as pltpu
from jax.sharding import PartitionSpec as P

F32 = jnp.float32
BF16 = jnp.bfloat16
MIB = 2**20
VM = pl.BlockSpec(memory_space=pltpu.VMEM)
SM = pl.BlockSpec(memory_space=pltpu.SMEM)
ANY = pl.BlockSpec(memory_space=pl.ANY)
HBM = pl.BlockSpec(memory_space=pltpu.HBM)
NT = (((1,), (1,)), ((), ()))
NX = 4


def place(y, x, c):
    return (y % 2) * 2 * NX + (x % NX) * 2 + c


def moves(step):
    return [
        (place(y, x, c), place(*step(y, x, c)))
        for y in range(2)
        for x in range(NX)
        for c in range(2)
    ]


UP = moves(lambda y, x, c: (y, x + 1, c))
DOWN = moves(lambda y, x, c: (y, x - 1, c))
ACROSS = moves(lambda y, x, c: (y + 1, x, c))
CORE = moves(lambda y, x, c: (y, x, 1 - c))


def send(array, pairs):
    return lax.ppermute(array, "view", pairs)


def params(mib):
    return pltpu.CompilerParams(vmem_limit_bytes=mib * MIB)


def split(value):
    high = value.astype(BF16)
    return high, (value - high.astype(F32)).astype(BF16)


def dot(a, b):
    return jnp.dot(a, b, preferred_element_type=F32)


def base_of(info, dx, dy, other, tiles):
    view = info[0]
    y, x, c = view // (2 * NX), (view // 2) % NX, view % 2
    c = 1 - c if other else c
    owner = lax.rem(y + dy, 2) * 2 * NX + lax.rem(x + dx + NX, NX) * 2 + c
    return owner * tiles


def cheap():
    return pl.CostEstimate(flops=1, bytes_accessed=1, transcendentals=0)


def round_volume(volume, info):
    def body(source, about, out):
        out[...] = source[...].astype(BF16)

    return pl.pallas_call(
        body,
        in_specs=[VM, SM],
        out_specs=VM,
        out_shape=jax.ShapeDtypeStruct(volume.shape, BF16),
        compiler_params=params(12),
        cost_estimate=cheap(),
        name="round_volume",
    )(volume, info)


def gate(arrays, after):
    n = len(arrays)

    def body(*refs):
        pass

    return pl.pallas_call(
        body,
        in_specs=[ANY] * (n + 1),
        out_specs=[ANY] * n,
        out_shape=[jax.ShapeDtypeStruct(a.shape, a.dtype) for a in arrays],
        input_output_aliases={i: i for i in range(n)},
        compiler_params=params(12),
        cost_estimate=cheap(),
        name="gate",
    )(*arrays, after)


def cut(array, start, size, after):
    def body(source, earlier, out):
        out[...] = source[:, start : start + size]

    return pl.pallas_call(
        body,
        in_specs=[VM, ANY],
        out_specs=VM,
        out_shape=jax.ShapeDtypeStruct((array.shape[0], size), array.dtype),
        compiler_params=params(12),
        cost_estimate=cheap(),
        name="cut",
    )(array, after)


def join(low, high, after):
    size = low.shape[1]

    def body(a, b, earlier, out):
        out[:, :size] = a[...]
        out[:, size:] = b[...]

    return pl.pallas_call(
        body,
        in_specs=[VM, VM, ANY],
        out_specs=VM,
        out_shape=jax.ShapeDtypeStruct((low.shape[0], 2 * size), low.dtype),
        compiler_params=params(12),
        cost_estimate=cheap(),
        name="join",
    )(low, high, after)


def load_footprints(source, after):
    pieces = 16
    each = source.shape[0] // pieces

    def body(src, earlier, target, sems):
        copies = [
            pltpu.make_async_copy(
                src.at[pl.ds(i * each, each)], target.at[pl.ds(i * each, each)], sems.at[i]
            )
            for i in range(pieces)
        ]
        for copy in copies:
            copy.start()
        for copy in copies:
            copy.wait()

    return pl.pallas_call(
        body,
        in_specs=[HBM, ANY],
        out_specs=VM,
        out_shape=pltpu.VMEM(source.shape, source.dtype),
        scratch_shapes=[pltpu.SemaphoreType.DMA((pieces,))],
        compiler_params=params(12),
        cost_estimate=pl.CostEstimate(flops=1, bytes_accessed=source.size * 2, transcendentals=0),
        name="load_footprints",
    )(source, after)


def placing(info, axial):
    most, planes = axial.shape
    window = 48
    first, length = info[1], info[2]
    live = lax.broadcasted_iota(jnp.int32, (most, planes), 0) < length
    masked = jnp.where(live, axial[...].astype(F32), 0.0).astype(BF16)
    hot = (
        lax.broadcasted_iota(jnp.int32, (window, most), 1) + first
        == lax.broadcasted_iota(jnp.int32, (window, most), 0)
    )
    return dot(jnp.where(hot, 1.0, 0.0).astype(BF16), masked)


def project(weights, blocks, info, places, shards, total=None, axial=None):
    planes, pixels = shards[0].shape
    width, columns = weights.shape[1], weights.shape[2]
    tiles = pixels // width
    detector = 8 * columns
    n = len(shards)
    started = total is not None
    last = axial is not None
    pieces = [
        (p, start, size)
        for p in range(n)
        for start, size in (((0, 4), (4, 4), (8, 8)) if p == 0 else ((0, 8), (8, 8)))
    ]

    def body(blk, about, w, *refs):
        refs = list(refs)
        parts = [refs.pop(0) for _ in range(n)]
        before = refs.pop(0) if started else None
        ax = refs.pop(0) if last else None
        outs = [refs.pop(0) for _ in range(3)] if last else None
        acc, slots, sems = refs
        origins = [base_of(about, *places[p], tiles) for p in range(n)]
        copies = [
            pltpu.make_async_copy(
                w.at[pl.ds(origins[p] + start, size)],
                slots.at[pl.ds(p * tiles + start, size)],
                sems.at[k],
            )
            for k, (p, start, size) in enumerate(pieces)
        ]
        for copy in copies:
            copy.start()
        acc[...] = before[...] if started else jnp.zeros(acc.shape, F32)
        for copy, (p, start, size) in zip(copies, pieces):
            copy.wait()
            for i in range(start, start + size):
                at = pl.multiple_of(blk[0, origins[p] + i] * columns, columns)
                row = parts[p][:, i * width : (i + 1) * width]
                acc[:, pl.ds(at, columns)] += dot(row, slots[p * tiles + i])
        if last:
            placed = placing(about, ax).astype(BF16)
            high, low = split(acc[...])
            spread = dot(placed, high) + dot(placed, low)
            outs[1][...] = spread[16:32]
            odd = lax.rem(about[3], 2)

            @pl.when(odd == 1)
            def _():
                outs[0][...] = spread[32:]
                outs[2][...] = spread[:16]

            @pl.when(odd == 0)
            def _():
                outs[0][...] = spread[:16]
                outs[2][...] = spread[32:]

    args = [blocks, info, weights, *shards]
    specs = [SM, SM, HBM] + [VM] * n
    if started:
        args.append(total)
        specs.append(VM)
    scratch = [
        pltpu.VMEM((n * tiles, width, columns), BF16),
        pltpu.SemaphoreType.DMA((len(pieces),)),
    ]
    if last:
        args.append(axial)
        specs.append(VM)
        out_shape = [jax.ShapeDtypeStruct((16, detector), F32)] * 3
        out_specs = [VM] * 3
        scratch = [pltpu.VMEM((planes, detector), F32)] + scratch
    else:
        out_shape = jax.ShapeDtypeStruct((planes, detector), F32)
        out_specs = VM
    return pl.pallas_call(
        body,
        in_specs=specs,
        out_specs=out_specs,
        out_shape=out_shape,
        scratch_shapes=scratch,
        compiler_params=params(2 * n + 4),
        cost_estimate=cheap(),
        name="project",
    )(*args)


def weigh(row_weight, sino, mine, low, high):
    def body(rw, measured, a, b, c, out, again, short):
        value = rw[0] * (measured[0] - (a[...] + b[...] + c[...]))
        out[...] = value
        again[...] = value
        short[...] = value.astype(BF16)

    return pl.pallas_call(
        body,
        in_specs=[VM] * 5,
        out_specs=[VM] * 3,
        out_shape=[jax.ShapeDtypeStruct(mine.shape, F32)] * 2
        + [
            jax.ShapeDtypeStruct(mine.shape, BF16),
        ],
        compiler_params=params(12),
        cost_estimate=cheap(),
        name="weigh",
    )(row_weight, sino, mine, low, high)


def smear(about, ax, rows, out):
    placed = placing(about, ax).T.astype(BF16)
    odd = lax.rem(about[3], 2) == 1
    first, second = rows[0][...].astype(F32), rows[2][...].astype(F32)
    low, high = jnp.where(odd, second, first), jnp.where(odd, first, second)
    high, low = split(jnp.concatenate([low, rows[1][...], high], axis=0))
    out[...] = (dot(placed, high) + dot(placed, low)).astype(BF16)


def pull(weights, blocks, info, places, smeared, after=(), out_dtype=F32, bands=None):
    width, columns = weights.shape[1], weights.shape[2]
    own = bands is not None
    given = list(bands) if own else [smeared]
    planes = bands[0].shape[1] if own else smeared.shape[0]
    tiles = weights.shape[0] // (4 * NX)
    pixels = tiles * width
    n = len(places)
    pieces = [
        (p, start, size)
        for p in range(n)
        for start, size in (((0, 4), (4, 4), (8, 8)) if p == 0 else ((0, 8), (8, 8)))
    ]

    def body(blk, about, w, *refs):
        args = refs[: len(given)]
        outs = refs[len(given) + len(after) : -2]
        slots, sems = refs[-2:]
        origins = [base_of(about, *places[p], tiles) for p in range(n)]
        copies = [
            pltpu.make_async_copy(
                w.at[pl.ds(origins[p] + start, size)],
                slots.at[pl.ds(p * tiles + start, size)],
                sems.at[k],
            )
            for k, (p, start, size) in enumerate(pieces)
        ]
        for copy in copies:
            copy.start()
        if own:
            sm = outs[n]
            smear(about, args[0], args[1:], sm)
        else:
            sm = args[0]
        for copy, (p, start, size) in zip(copies, pieces):
            copy.wait()
            for i in range(start, start + size):
                at = pl.multiple_of(blk[0, origins[p] + i] * columns, columns)
                value = lax.dot_general(
                    sm[:, pl.ds(at, columns)],
                    slots[p * tiles + i],
                    NT,
                    preferred_element_type=F32,
                )
                outs[p][:, i * width : (i + 1) * width] = value.astype(out_dtype)

    out_shape = [jax.ShapeDtypeStruct((planes, pixels), out_dtype)] * n
    if own:
        out_shape.append(jax.ShapeDtypeStruct((planes, bands[1].shape[1]), BF16))
    return pl.pallas_call(
        body,
        in_specs=[SM, SM, HBM] + [VM] * len(given) + [ANY] * len(after),
        out_specs=[VM] * len(out_shape),
        out_shape=out_shape,
        scratch_shapes=[
            pltpu.VMEM((n * tiles, width, columns), BF16),
            pltpu.SemaphoreType.DMA((len(pieces),)),
        ],
        compiler_params=params(24),
        cost_estimate=cheap(),
        name="pull",
    )(blocks, info, weights, *given, *after)


def combine(sums, size, cuts=1, after=()):
    arrays = list({id(term[0]): term[0] for terms in sums for term in terms}.values())
    half = size // 2
    planes = arrays[0].shape[0]

    def body(*refs):
        given = dict(zip([id(a) for a in arrays], refs[: len(arrays)]))
        outs = refs[len(arrays) + len(after) :]
        for s, terms in enumerate(sums):
            for h in range(2):
                value = None
                for array, first, halves in terms:
                    if h in halves:
                        first += h * half
                        more = given[id(array)][:, first : first + half].astype(F32)
                        value = more if value is None else value + more
                if cuts == 2:
                    outs[2 * s + h][...] = value.astype(BF16)
                else:
                    outs[s][:, h * half : (h + 1) * half] = value.astype(BF16)

    return pl.pallas_call(
        body,
        in_specs=[VM] * len(arrays) + [ANY] * len(after),
        out_specs=[VM] * (len(sums) * cuts),
        out_shape=[jax.ShapeDtypeStruct((planes, size // cuts), BF16)] * (len(sums) * cuts),
        compiler_params=params(16),
        cost_estimate=cheap(),
        name="combine",
    )(*arrays, *after)


def update(volume, col_weight, kept, swap, arrived):
    def body(vol, weight, mine, d, a, b, c, out):
        summed = mine[...] + d[...].astype(F32) + a[...].astype(F32) + b[...].astype(F32) + c[...].astype(F32)
        out[...] = jnp.maximum(vol[...] + weight[...] * summed, 0.0)

    planes, pixels = volume.shape
    block = pl.BlockSpec((planes, pixels // 2), lambda i: (0, i))
    return pl.pallas_call(
        body,
        grid=(2,),
        in_specs=[block] * 7,
        out_specs=block,
        out_shape=jax.ShapeDtypeStruct(volume.shape, F32),
        compiler_params=params(12),
        name="update",
    )(
        volume,
        col_weight,
        kept,
        swap,
        *arrived,
    )


def per_device(
    volume, sino, transaxial, blocks, axial, band_start, band_len, row_weight, col_weight
):
    planes, pixels = volume.shape
    rows_here = sino.shape[1]
    half = pixels // 2
    ax = jnp.swapaxes(axial[0], 0, 1)
    slab = lax.axis_index("slab")
    view = lax.axis_index("view")
    first = band_start[0, 0] - (slab - 1) * rows_here
    info = jnp.stack([view, first, band_len[0, 0], slab]).astype(jnp.int32)

    def whose(dx, dy):
        return [(dx, dy, False), (dx, dy, True)]

    own = round_volume(volume, info)
    left = send(own, UP)
    right = send(own, DOWN)
    over = send(own, ACROSS)
    swapped = send(own, CORE)
    weights = pltpu.with_memory_space_constraint(transaxial[0], pltpu.HBM)
    ahead = functools.partial(project, weights, blocks, info)
    total = ahead(whose(0, 0), [own, swapped])
    left, right = gate([left, right], total)
    (over,) = gate([over], left)
    far_low = send(cut(left, 0, half, total), UP)
    far_high = send(cut(right, half, half, total), DOWN)
    left_over = send(over, UP)
    right_over = send(over, DOWN)
    total = ahead(
        whose(-1, 0) + whose(1, 0), [left, send(left, CORE), right, send(right, CORE)], total
    )
    far = join(far_low, far_high, total)
    far_over = send(far, ACROSS)
    far_swapped = send(far, CORE)
    total = ahead(whose(0, 1) + [(2, 0, False)], [over, send(over, CORE), far], total)
    left_over, right_over = gate([left_over, right_over], total)
    total = ahead(
        [(2, 0, True), (-1, 1, False), (1, 1, False)],
        [far_swapped, left_over, right_over],
        total,
    )
    left_swapped, right_swapped = send(left_over, CORE), send(right_over, CORE)
    (far_over,) = gate([far_over], total)
    to_first, mine, to_second = ahead(
        [(-1, 1, True), (1, 1, True)] + whose(2, 1),
        [left_swapped, right_swapped, far_over, send(far_over, CORE)],
        total,
        ax,
    )

    count = lax.axis_size("slab")
    first_swap, second_swap = (
        [(a, b) for i in range(start, count - 1, 2) for a, b in ((i, i + 1), (i + 1, i))]
        for start in (1, 0)
    )
    residual, own_rows, rounded = weigh(
        row_weight,
        sino,
        mine,
        lax.ppermute(to_first, "slab", first_swap),
        lax.ppermute(to_second, "slab", second_swap),
    )
    first_rows = lax.ppermute(rounded, "slab", first_swap)
    second_rows = lax.ppermute(rounded, "slab", second_swap)

    back = functools.partial(pull, weights, blocks, info)
    full = (0, 1)

    def others(*offsets):
        return [(dx, dy, True) for dx, dy in offsets]

    def owns(*offsets):
        return [(dx, dy, False) for dx, dy in offsets]

    def swap_parts(offsets, after):
        parts = back(others(*offsets), smeared, after=after, out_dtype=BF16)
        return parts[0], [send(part, CORE) for part in parts]

    def whole(array):
        return (array, 0, full)

    offsets = [(2, 1), (1, 1), (-1, 1)]
    *parts, smeared = back(
        others(*offsets), None, out_dtype=BF16, bands=[ax, first_rows, own_rows, second_rows]
    )
    swaps = [send(part, CORE) for part in parts]
    part = parts[0]
    mine = back(owns(*offsets), smeared, after=[part])
    far_sum, up_sum, down_sum = combine([[whole(a), whole(b)] for a, b in zip(mine, swaps)], pixels)
    from_over = send(far_sum, ACROSS)
    from_left = send(up_sum, UP)
    from_right = send(down_sum, DOWN)
    offsets = [(2, 0), (0, 1)]
    part, swaps = swap_parts(offsets, [far_sum])
    mine = back(owns(*offsets), smeared, after=[part])
    offsets = [(1, 0), (-1, 0), (0, 0)]
    part, last_swaps = swap_parts(offsets, [mine[0]])
    from_left, from_right, from_over = gate([from_left, from_right, from_over], part)
    swaps = gate(swaps, from_over)
    half_up, half_down = combine([[whole(mine[0]), whole(swaps[0]), whole(from_over)]], pixels, 2)
    half_left = send(half_up, UP)
    half_right = send(half_down, DOWN)
    (over_sum,) = combine(
        [[whole(mine[1]), whole(swaps[1]), whole(from_left), whole(from_right)]],
        pixels,
        after=[half_up],
    )
    over_last = send(over_sum, ACROSS)
    mine = back(owns(*offsets), smeared, after=[over_sum])
    half_left, half_right = gate([half_left, half_right], mine[0])
    swaps = gate(last_swaps, half_left)
    up_sum, down_sum = combine(
        [
            [whole(mine[0]), whole(swaps[0]), (half_left, 0, (0,))],
            [whole(mine[1]), whole(swaps[1]), (half_right, -half, (1,))],
        ],
        pixels,
    )
    left_last = send(up_sum, UP)
    right_last = send(down_sum, DOWN)
    updated = update(
        volume, col_weight, mine[2], swaps[2], [over_last, left_last, right_last]
    )
    return updated, residual[None]


def solution(mesh):
    in_specs = (
        P("slab", "view"),
        P("view", "slab", None),
        P("view", None, None, None),
        P("view", None),
        P("view", "slab", None),
        P("view", "slab"),
        P("view", "slab"),
        P("view", "slab", None),
        P("slab", "view"),
    )
    out_specs = (P("slab", "view"), P("view", "slab", None))
    return jax.shard_map(
        per_device, mesh=mesh, in_specs=in_specs, out_specs=out_specs, check_vma=False
    )
```
